1024 devices in a mesh: row: 32 (over z), col: 8 (over x, core), layer: 4 (over y).
Axes of the slice: x: 4, y: 4, z: 32, core: 2. Of those that a mesh axis runs over, the one named last changes fastest.
Arguments:
- a_tiles: bfloat16 [8, 32, 4, 3, 128, 128], P('col', 'row', 'layer'), may hold values from -6 to 6
- a_occ: int32 [8, 32, 4, 3], P('col', 'row', 'layer'), may hold values from 0 to 1, as said below
- b_tiles: bfloat16 [32, 4, 32, 3, 128, 128], P('col', 'layer', 'row'), may hold values from -0.046875 to 0.046875
- b_occ: int32 [32, 4, 32, 3], P('col', 'layer', 'row'), may hold values from 0 to 1, as said below
- stacks: int32 [8, 32, 4, 32, 8, 3], P('col', 'row', 'layer'), may hold values from 0 to 3, as said below
- stack_count: int32 [8, 32, 4, 32], P('col', 'row', 'layer'), may hold values from 1 to 8, as said below
- c_keep: int32 [8, 32, 4], P('col', 'row', 'layer'), may hold values 0 or 1
Outputs:
- c_out: bfloat16 [8, 32, 4, 128, 128], P('col', 'row', 'layer')
The draws below stay inside these ranges and needn't reach their ends.
Inputs may be any that keep to these rules, and one draw needn't show every extreme that they name: `a_occ`: 0 or 1; how full a panel is varies from panel to panel. `b_occ`: 0 or 1; how full a panel is varies from panel to panel. `stacks`: left slot s below 3 lies in row block s % 2, right slot t below 3 in column block t % 2, and the product slot is 2 * (s % 2) + (t % 2); the entries of one stack name distinct (left, right) pairs; the largest product slot occurs. `stack_count`: entries at and past the count are padding and are ignored; the largest count occurs in every draw.
All inputs are finite; a program needn't handle non-finite values. No bound on the sum of `c_keep` on one device may be relied on, other than what follows from the above.
Results may differ from the reference program's by a relative error of at most 0.001.
Values may be sent and summed in bfloat16 or wider, within the bound.
No kernel may reach another device: no remote copies, remote signals or barrier semaphores. Data moves between devices by JAX's collectives and lax.ppermute only.
A program may use at most 32 MiB of HBM per device.

```python
import jax
import jax.numpy as jnp
from jax import lax

TILE = 128
SA = 3
SB = 3
SC = 4
STACK = 8
N_ROW = 32
N_COL = 8
N_LAYER = 4


def occupancy(key, shape):
    k_level, k_bits = jax.random.split(key, 2)
    level = jax.random.randint(k_level, shape[:-1] + (1,), 0, 4)
    bits = jax.random.randint(k_bits, shape, 0, 4)
    return (bits <= level).astype(jnp.int32)


def draw_a_occ(key, part):
    key = jax.random.fold_in(key, 3)
    return occupancy(key, (N_COL, N_ROW, N_LAYER, SA))


def draw_b_occ(key, part):
    key = jax.random.fold_in(key, 5)
    return occupancy(key, (N_ROW, N_LAYER, N_ROW, SB))


def draw_stacks(key, part):
    key = jax.random.fold_in(key, 11)
    k_score, k_spot = jax.random.split(key, 2)
    n_pairs = SA * SB
    panels = N_COL * N_ROW * N_LAYER * N_ROW
    scores = jax.random.randint(k_score, (panels, n_pairs), 0, 1 << 20) * n_pairs
    scores = scores + jnp.arange(n_pairs, dtype=jnp.int32)[None, :]
    spot = jax.random.randint(k_spot, (), 0, panels)
    scores = scores.at[spot, SB + 1].set(-1)
    order = jnp.argsort(scores, axis=1, stable=True)[:, :STACK].astype(jnp.int32)
    left = order // SB
    right = order % SB
    target = 2 * (left % 2) + right % 2
    triples = jnp.stack([left, right, target], -1)
    return triples.reshape((N_COL, N_ROW, N_LAYER, N_ROW, STACK, 3)).astype(jnp.int32)


def draw_stack_count(key, part):
    key = jax.random.fold_in(key, 7)
    k_level, k_spread, k_spot = jax.random.split(key, 3)
    shape = (N_COL, N_ROW, N_LAYER, N_ROW)
    level = jax.random.randint(k_level, (N_COL, N_ROW, N_LAYER, 1), 1, 5)
    spread = jax.random.randint(k_spread, shape, 0, STACK)
    counts = jnp.minimum(1 + spread * level // 4, STACK).reshape(-1)
    spot = jax.random.randint(k_spot, (), 0, counts.shape[0])
    counts = counts.at[spot].set(STACK)
    return counts.reshape(shape).astype(jnp.int32)


def with_ends(array, key, least, high):
    longest = array.shape.index(max(array.shape))
    spots = []
    for shift in (0, 1):
        where = [jax.random.randint(jax.random.fold_in(key, axis), (), 0, length) for axis, length in enumerate(array.shape)]
        where[longest] = (where[longest] + shift) % array.shape[longest]
        spots.append(tuple(where))
    return array.at[spots[0]].set(least).at[spots[1]].set(high)


def level_of(own_key, shape, cuts, low, top_value):
    level, own = 1.0, jax.random.fold_in(own_key, 6)
    for axis_at, blocks in cuts:
        heights = jnp.exp(jax.random.uniform(jax.random.fold_in(own, axis_at), (blocks,), jnp.float32, low / len(cuts), top_value / len(cuts)))
        level = level * jnp.repeat(heights, shape[axis_at] // blocks).reshape([-1 if axis == axis_at else 1 for axis in range(len(shape))])
    return level


def bell_draw(own_key, shape, deviation, bound, pieces=(), kind=jnp.bfloat16):
    gain = level_of(own_key, shape, pieces, -0.22, 0.18) if pieces else 1.0
    values = jax.random.normal(own_key, shape, jnp.float32) * deviation * gain
    return jnp.minimum(jnp.maximum(values, -bound), bound).astype(kind)


def setup_inputs(seed: int = 0) -> dict:
    streams_of = jax.random.split(jax.random.key(seed), 8)
    return {
        "a_tiles": bell_draw(streams_of[0], (N_COL, N_ROW, N_LAYER, SA, TILE, TILE), 1.0, 6.0, ((0, 8), (1, 32), (2, 4))),
        "a_occ": draw_a_occ(jax.random.fold_in(streams_of[7], 71), 0),
        "b_tiles": bell_draw(streams_of[2], (N_ROW, N_LAYER, N_ROW, SB, TILE, TILE), (TILE * N_ROW * N_LAYER * STACK // (2 * SC)) ** -0.5, 0.046875, ((0, 8), (1, 4), (2, 32))),
        "b_occ": draw_b_occ(jax.random.fold_in(streams_of[7], 71), 0),
        "stacks": draw_stacks(jax.random.fold_in(streams_of[7], 71), 0),
        "stack_count": draw_stack_count(jax.random.fold_in(streams_of[7], 71), 0),
        "c_keep": with_ends((jax.random.randint(streams_of[6], (N_COL, N_ROW, SC), 0, 4) < 3).astype(jnp.int32), jax.random.fold_in(streams_of[6], 1), 0, 1),
    }


def reference(a_tiles, a_occ, b_tiles, b_occ, stacks, stack_count, c_keep):
    a_held = a_tiles.astype(jnp.float32) * a_occ.astype(jnp.float32)[..., None, None]
    b_held = b_tiles.astype(jnp.float32) * b_occ.astype(jnp.float32)[..., None, None]
    entries = N_LAYER * N_ROW

    def pair_block(position):
        prow = position // N_ROW
        pcol = position % N_ROW
        triples = stacks[prow, pcol].reshape(entries, STACK, 3)
        counts = stack_count[prow, pcol].reshape(entries)
        left = jnp.swapaxes(a_held[prow], 0, 1).reshape(entries, SA, TILE, TILE)
        right = jnp.swapaxes(b_held[:, :, pcol], 0, 1).reshape(entries, SB, TILE, TILE)
        rows_idx = jnp.arange(entries, dtype=jnp.int32)[:, None]
        left_sel = left[rows_idx, triples[:, :, 0]]
        right_sel = right[rows_idx, triples[:, :, 1]]
        products = jnp.einsum("esij,esjk->esik", left_sel, right_sel, precision=lax.Precision.HIGHEST)
        target = triples[:, :, 2][:, :, None] == jnp.arange(SC, dtype=jnp.int32)[None, None, :]
        live = jnp.arange(STACK, dtype=jnp.int32)[None, :, None] < counts[:, None, None]
        weights = (target & live).astype(jnp.float32)
        summed = jnp.einsum("esc,esik->cik", weights, products, precision=lax.Precision.HIGHEST)
        return summed * c_keep[prow, pcol].astype(jnp.float32)[:, None, None]

    result = lax.map(pair_block, jnp.arange(N_COL * N_ROW, dtype=jnp.int32))
    return result.reshape(N_COL, N_ROW, SC, TILE, TILE).astype(jnp.bfloat16)
```

```python
import jax
import jax.numpy as jnp
from jax import lax
from jax.experimental import pallas as pl
from jax.experimental.pallas import tpu as pltpu
from jax.sharding import Mesh, PartitionSpec as P

TILE = 128
LEFT = 3
RIGHT = 3
PANEL = LEFT * TILE
W_ROWS = 16


def encode(values):
    size = jnp.abs(values)
    least = 2.0**-126
    exponent = jnp.floor(jnp.log(jnp.maximum(size, least)) * 1.4426950408889634)
    exponent = jnp.maximum(exponent, -126.0)
    scaled = size * jnp.exp2(-exponent)
    code = jnp.floor((exponent + 126.0 + scaled) * 128.0 + 0.5)
    code = jnp.where(size < least, 0.0, code)
    return jnp.where(values < 0, -code, code).astype(jnp.int32).astype(jnp.int16)


def decode(codes):
    wide = codes.astype(jnp.int32)
    size = jnp.abs(wide)
    power = jnp.exp2(((size >> 7) - 127).astype(jnp.float32))
    value = (1.0 + (size & 127).astype(jnp.float32) * (1.0 / 128.0)) * power
    value = jnp.where(size < 128, 0.0, value)
    return jnp.where(wide < 0, -value, value).astype(jnp.bfloat16)


def prepare(a_ref, a_occ, b_ref, b_occ, stacks, counts, code_ref, send_ref, w_scr):
    for s in range(LEFT):
        held = a_ref[s].astype(jnp.float32) * a_occ[0, 0, 0, s].astype(jnp.float32)
        code_ref[s] = encode(held)
    for panel in range(4):
        for t in range(RIGHT):
            bit = b_occ[panel, 0, 0, t]
            row = (panel // 2) * PANEL + t * TILE
            tile = b_ref[panel, t]
            send_ref[panel % 2, row : row + TILE] = jnp.where(bit > 0, tile, jnp.zeros_like(tile))
    lanes = lax.broadcasted_iota(jnp.int32, (8, TILE), 1)
    entries = lax.broadcasted_iota(jnp.int32, (8, TILE), 0)
    for k in range(32):
        triple = stacks[k]
        pair = triple[:, 0:1] * RIGHT + triple[:, 1:2]
        hit = (jnp.broadcast_to(pair, (8, TILE)) == lanes) & (entries < counts[0, 0, 0, k])
        w_scr[k % 2, k // 2] = jnp.sum(jnp.where(hit, 1.0, 0.0), axis=0)
    send_ref[:, 2 * PANEL :] = w_scr[...].astype(jnp.bfloat16)


def products(code_ref, b_ref, w_ref, out_ref, w_scr):
    step = pl.program_id(0)

    @pl.when(step == 0)
    def _():
        out_ref[...] = jnp.zeros_like(out_ref)
        w_scr[...] = w_ref[...].astype(jnp.float32)

    def weighted(at, q, s, t):
        row = w_scr[q, pl.ds(2 * step + at, 1), :]
        weight = jnp.broadcast_to(row[:, s * RIGHT + t : s * RIGHT + t + 1], (16, TILE)).astype(jnp.bfloat16)
        tile = b_ref[0, q, at * PANEL + t * TILE : at * PANEL + (t + 1) * TILE]
        return (tile.reshape(8, 16, TILE) * weight[None]).reshape(TILE, TILE)

    left = [[decode(code_ref[at, s]) for s in range(LEFT)] for at in range(2)]
    for block, members in ((0, (0, 2)), (1, (1,))):
        lhs = jnp.concatenate([left[at][s] for at in range(2) for s in members], axis=1)
        extra = []
        for q in range(2):
            rhs = jnp.concatenate(
                [
                    jnp.concatenate([weighted(at, q, s, 0), weighted(at, q, s, 1)], axis=1)
                    for at in range(2)
                    for s in members
                ],
                axis=0,
            )
            both = jnp.dot(lhs, rhs, preferred_element_type=jnp.float32)
            out_ref[2 * block, q] += both[:, :TILE]
            out_ref[2 * block + 1, q] += both[:, TILE:]
            extra.append(
                jnp.concatenate([weighted(at, q, s, 2) for at in range(2) for s in members], axis=0)
            )
        both = jnp.dot(lhs, jnp.concatenate(extra, axis=1), preferred_element_type=jnp.float32)
        out_ref[2 * block, 0] += both[:, :TILE]
        out_ref[2 * block, 1] += both[:, TILE:]


def local(a_tiles, a_occ, b_tiles, b_occ, stacks, stack_count, c_keep):
    vmem = pl.BlockSpec(memory_space=pltpu.VMEM)
    smem = pl.BlockSpec(memory_space=pltpu.SMEM)
    codes, send = pl.pallas_call(
        prepare,
        out_shape=(
            jax.ShapeDtypeStruct((LEFT, TILE, TILE), jnp.int16),
            jax.ShapeDtypeStruct((2, 2 * PANEL + W_ROWS, TILE), jnp.bfloat16),
        ),
        in_specs=[vmem, smem, vmem, smem, vmem, smem],
        out_specs=(vmem, vmem),
        scratch_shapes=[pltpu.VMEM((2, W_ROWS, TILE), jnp.float32)],
        name="prepare",
    )(a_tiles[0, 0, 0], a_occ, b_tiles[:, 0, 0], b_occ, stacks[0, 0, 0], stack_count)
    pair = lax.all_to_all(send, "row_low", 0, 0, tiled=True)
    right_all = lax.all_gather(pair, "col", axis=0)
    left_all = lax.all_gather(codes, "row_high", axis=0)
    n_cols = right_all.shape[0]
    partial = pl.pallas_call(
        products,
        grid=(n_cols,),
        out_shape=jax.ShapeDtypeStruct((4, 2, TILE, TILE), jnp.float32),
        in_specs=[
            pl.BlockSpec((2, LEFT, TILE, TILE), lambda g: (g, 0, 0, 0)),
            pl.BlockSpec((1, 2, 2 * PANEL, TILE), lambda g: (g, 0, 0, 0)),
            pl.BlockSpec((2, W_ROWS, TILE), lambda g: (0, 2 * PANEL // W_ROWS, 0)),
        ],
        out_specs=pl.BlockSpec((4, 2, TILE, TILE), lambda g: (0, 0, 0, 0)),
        scratch_shapes=[pltpu.VMEM((2, W_ROWS, TILE), jnp.float32)],
        compiler_params=pltpu.CompilerParams(vmem_limit_bytes=24 * 1024 * 1024),
        name="products",
    )(left_all, right_all, pair)
    shares = lax.all_to_all(
        partial.reshape(8, TILE, TILE), ("layer", "row_low"), 0, 0, tiled=True
    )
    kept = jnp.sum(shares, axis=0) * c_keep[0, 0, 0].astype(jnp.float32)
    return kept.astype(jnp.bfloat16)[None, None, None]


def solution(mesh):
    rows, cols, layers = (mesh.shape[name] for name in ("row", "col", "layer"))
    paired = Mesh(
        mesh.devices.reshape(rows // 2, 2, cols, layers), ("row_high", "row_low", "col", "layer")
    )
    row = ("row_high", "row_low")
    return jax.shard_map(
        local,
        mesh=paired,
        in_specs=(
            P("col", row, "layer", None, None, None),
            P("col", row, "layer", None),
            P("col", "layer", row, None, None, None),
            P("col", "layer", row, None),
            P("col", row, "layer", None, None, None),
            P("col", row, "layer", None),
            P("col", row, "layer"),
        ),
        out_specs=P("col", row, "layer", None, None),
        check_vma=False,
    )
```

```python
import jax
import jax.numpy as jnp
from jax import lax
from jax.experimental import pallas as pl
from jax.experimental.pallas import tpu as pltpu
from jax.sharding import Mesh, PartitionSpec as P

TILE = 128
LEFT = 3
RIGHT = 3
PANEL = LEFT * TILE
W_ROWS = 16
BLOCK = 2 * PANEL + W_ROWS


def encode(values):
    size = jnp.abs(values)
    least = 2.0**-124
    exponent = jnp.floor(jnp.log(jnp.maximum(size, least)) * 1.4426950408889634)
    scaled = size * jnp.exp2(-exponent)
    exponent = jnp.where(scaled >= 1.996, exponent + 1.0, jnp.where(scaled < 0.998, exponent - 1.0, exponent))
    exponent = jnp.maximum(exponent, -124.0)
    significand = jnp.floor(size * jnp.exp2(-exponent) * 128.0 + 0.5)
    significand = jnp.where(values < 0, -significand, significand)
    code = jnp.where(size < least, 0.0, (exponent + 61.0) * 512.0 + significand)
    return code.astype(jnp.int32).astype(jnp.int16)


def decode(codes):
    scaled = codes.astype(jnp.int32).astype(jnp.float32) * (1.0 / 128.0)
    exponent = jnp.floor(scaled * 0.25 + 0.5)
    return ((scaled - 4.0 * exponent) * jnp.exp2(exponent - 61.0)).astype(jnp.bfloat16)


def right_block(low, parity, b_ref, b_occ, block):
    for half in range(2):
        for t in range(RIGHT):
            row = half * PANEL + t * TILE
            panel = 2 * half + parity
            tile = b_ref[panel, t]
            block[row : row + TILE] = jnp.where(b_occ[0, t, 0, panel] > 0, tile, jnp.zeros_like(tile))


def stack_weights(stacks, counts):
    pair = stacks[0] * RIGHT + stacks[1]
    live = lax.broadcasted_iota(jnp.int32, pair.shape, 0) < counts[0, 0]
    rows = lax.broadcasted_iota(jnp.int32, (W_ROWS, pair.shape[1]), 0)
    weights = jnp.zeros(rows.shape, jnp.float32)
    for number in range(LEFT * RIGHT):
        used = jnp.where(live & (pair == number), 1.0, 0.0)
        weights = jnp.where(rows == number, jnp.sum(used, axis=0, keepdims=True), weights)
    return jnp.concatenate([weights] * (TILE // pair.shape[1]), axis=1)


def put_weights(parity, weights, block):
    shifted = jnp.concatenate([weights[:, 1:], weights[:, :1]], axis=1)
    block[2 * PANEL :] = jnp.where(parity == 0, weights, shifted).astype(jnp.bfloat16)


def copy_all(source, out_ref, slot, sems):
    copies = [
        pltpu.make_async_copy(source, out_ref.at[at, slot], sems.at[at]) for at in range(out_ref.shape[0])
    ]
    for copy in copies:
        copy.start()
    return copies


def prepare_other(low_ref, b_ref, b_occ, stacks, counts, send_ref):
    low = low_ref[0]
    put_weights(1 - low, stack_weights(stacks, counts), send_ref)
    right_block(low, 1 - low, b_ref, b_occ, send_ref)


def prepare_own(low_ref, b_ref, b_occ, stacks, counts, a_ref, a_occ, out_ref, code_ref, own, sems):
    low = low_ref[0]
    put_weights(low, stack_weights(stacks, counts), own)
    right_block(low, low, b_ref, b_occ, own)
    copies = copy_all(own, out_ref, low, sems)
    for s in range(LEFT):
        held = a_ref[s].astype(jnp.float32) * a_occ[0, 0, 0, s].astype(jnp.float32)
        code_ref[0, s * TILE : (s + 1) * TILE] = encode(held)
    for copy in copies:
        copy.wait()


def add_other(low_ref, other, _, out_ref, sems):
    for copy in copy_all(other, out_ref, 1 - low_ref[0], sems):
        copy.wait()


def products(col_ref, code_ref, b_ref, out_ref):
    n_cols = b_ref.shape[0]
    out_ref[...] = jnp.zeros_like(out_ref)
    lanes = lax.broadcasted_iota(jnp.int32, (W_ROWS, TILE), 1)
    weights = [b_ref[col_ref[0], q, 2 * PANEL :].astype(jnp.float32) for q in range(2)]

    for g in range(n_cols):
        chosen = [
            [
                jnp.sum(jnp.where(lanes == 2 * (2 * g + at), weights[q], 0.0), axis=1, keepdims=True)
                for q in range(2)
            ]
            for at in range(2)
        ]

        def weighted(at, q, s, t):
            number = s * RIGHT + t
            weight = jnp.broadcast_to(chosen[at][q][number : number + 1], (16, TILE)).astype(jnp.bfloat16)
            row = at * PANEL + t * TILE
            tile = b_ref[g, q, row : row + TILE]
            return (tile.reshape(8, 16, TILE) * weight[None]).reshape(TILE, TILE)

        left = [
            [decode(code_ref[2 * g + at, s * TILE : (s + 1) * TILE]) for s in range(LEFT)]
            for at in range(2)
        ]
        for block, members in ((0, (0, 2)), (1, (1,))):
            lhs = jnp.concatenate([left[at][s] for at in range(2) for s in members], axis=1)
            extra = []
            for q in range(2):
                rhs = jnp.concatenate(
                    [
                        jnp.concatenate([weighted(at, q, s, 0), weighted(at, q, s, 1)], axis=1)
                        for at in range(2)
                        for s in members
                    ],
                    axis=0,
                )
                both = jnp.dot(lhs, rhs, preferred_element_type=jnp.float32)
                out_ref[2 * block, q] += both[:, :TILE]
                out_ref[2 * block + 1, q] += both[:, TILE:]
                extra.append(
                    jnp.concatenate([weighted(at, q, s, 2) for at in range(2) for s in members], axis=0)
                )
            both = jnp.dot(lhs, jnp.concatenate(extra, axis=1), preferred_element_type=jnp.float32)
            out_ref[2 * block, 0] += both[:, :TILE]
            out_ref[2 * block, 1] += both[:, TILE:]


def local(a_tiles, a_occ, b_tiles, b_occ, stacks, stack_count, c_keep):
    n_cols = lax.axis_size("col")
    vmem = pl.BlockSpec(memory_space=pltpu.VMEM)
    smem = pl.BlockSpec(memory_space=pltpu.SMEM)
    hbm = pl.BlockSpec(memory_space=pltpu.HBM)
    low = lax.axis_index("row_low").reshape(1)
    spread = jax.ShapeDtypeStruct((n_cols, 2, BLOCK, TILE), jnp.bfloat16)
    right_args = (
        b_tiles[:, 0, 0],
        b_occ.transpose(1, 3, 2, 0),
        stacks[0, 0, 0].transpose(2, 1, 0),
        stack_count,
    )
    send = pl.pallas_call(
        prepare_other,
        out_shape=jax.ShapeDtypeStruct((BLOCK, TILE), jnp.bfloat16),
        in_specs=[smem, vmem, smem, vmem, vmem],
        out_specs=vmem,
        name="prepare_other",
    )(low, *right_args)
    other = lax.ppermute(send, "row_low", [(0, 1), (1, 0)])
    right, codes = pl.pallas_call(
        prepare_own,
        out_shape=(spread, jax.ShapeDtypeStruct((1, PANEL, TILE), jnp.int16)),
        in_specs=[smem, vmem, smem, vmem, vmem, vmem, smem],
        out_specs=(hbm, vmem),
        scratch_shapes=[pltpu.VMEM((BLOCK, TILE), jnp.bfloat16), pltpu.SemaphoreType.DMA((n_cols,))],
        cost_estimate=pl.CostEstimate(flops=10_000_000, bytes_accessed=4_000_000, transcendentals=0),
        name="prepare_own",
    )(low, *right_args, a_tiles[0, 0, 0], a_occ)
    other, right, codes = lax.optimization_barrier((other, right, codes))
    right = pl.pallas_call(
        add_other,
        out_shape=spread,
        in_specs=[smem, vmem, hbm],
        out_specs=hbm,
        scratch_shapes=[pltpu.SemaphoreType.DMA((n_cols,))],
        input_output_aliases={2: 0},
        compiler_params=pltpu.CompilerParams(vmem_limit_bytes=54_000_000),
        name="add_other",
    )(low, other, right)
    right_all = lax.all_to_all(right, "col", 0, 0, tiled=True)
    left_all = lax.all_gather(codes, "row_high", axis=0, tiled=True)
    partial = pl.pallas_call(
        products,
        out_shape=jax.ShapeDtypeStruct((4, 2, TILE, TILE), jnp.float32),
        in_specs=[smem, vmem, vmem],
        out_specs=vmem,
        compiler_params=pltpu.CompilerParams(vmem_limit_bytes=16 * 1024 * 1024),
        name="products",
    )(lax.axis_index("col").reshape(1), left_all, right_all)
    shares = lax.all_to_all(
        partial.reshape(8, TILE, TILE), ("layer", "row_low"), 0, 0, tiled=True
    )
    kept = jnp.sum(shares, axis=0) * c_keep[0, 0, 0].astype(jnp.float32)
    return kept.astype(jnp.bfloat16)[None, None, None]


def solution(mesh):
    rows, cols, layers = (mesh.shape[name] for name in ("row", "col", "layer"))
    paired = Mesh(
        mesh.devices.reshape(rows // 2, 2, cols, layers), ("row_high", "row_low", "col", "layer")
    )
    row = ("row_high", "row_low")
    return jax.shard_map(
        local,
        mesh=paired,
        in_specs=(
            P("col", row, "layer", None, None, None),
            P("col", row, "layer", None),
            P("col", "layer", row, None, None, None),
            P("col", "layer", row, None),
            P("col", row, "layer", None, None, None),
            P("col", row, "layer", None),
            P("col", row, "layer"),
        ),
        out_specs=P("col", row, "layer", None, None),
        check_vma=False,
    )
```

```python
import jax
import jax.numpy as jnp
from jax import lax
from jax.experimental import pallas as pl
from jax.experimental.pallas import tpu as pltpu
from jax.sharding import Mesh, PartitionSpec as P

TILE = 128
LEFT = 3
RIGHT = 3
PANEL = LEFT * TILE
W_ROWS = 16
BLOCK = 2 * PANEL + W_ROWS


def encode(values):
    size = jnp.abs(values)
    least = 2.0**-124
    exponent = jnp.floor(jnp.log(jnp.maximum(size, least)) * 1.4426950408889634)
    scaled = size * jnp.exp2(-exponent)
    exponent = jnp.where(scaled >= 1.996, exponent + 1.0, jnp.where(scaled < 0.998, exponent - 1.0, exponent))
    exponent = jnp.maximum(exponent, -124.0)
    significand = jnp.floor(size * jnp.exp2(-exponent) * 128.0 + 0.5)
    significand = jnp.where(values < 0, -significand, significand)
    code = jnp.where(size < least, 0.0, (exponent + 61.0) * 512.0 + significand)
    return code.astype(jnp.int32).astype(jnp.int16)


def decode(codes):
    scaled = codes.astype(jnp.int32).astype(jnp.float32) * (1.0 / 128.0)
    exponent = jnp.floor(scaled * 0.25 + 0.5)
    return ((scaled - 4.0 * exponent) * jnp.exp2(exponent - 61.0)).astype(jnp.bfloat16)


def right_block(low, parity, b_ref, b_occ, block):
    for half in range(2):
        for t in range(RIGHT):
            row = half * PANEL + t * TILE
            panel = 2 * half + parity
            tile = b_ref[panel, t]
            block[row : row + TILE] = jnp.where(b_occ[0, t, 0, panel] > 0, tile, jnp.zeros_like(tile))


def stack_weights(stacks, counts):
    pair = stacks[0] * RIGHT + stacks[1]
    live = lax.broadcasted_iota(jnp.int32, pair.shape, 0) < counts[0, 0]
    rows = lax.broadcasted_iota(jnp.int32, (W_ROWS, pair.shape[1]), 0)
    weights = jnp.zeros(rows.shape, jnp.float32)
    for number in range(LEFT * RIGHT):
        used = jnp.where(live & (pair == number), 1.0, 0.0)
        weights = jnp.where(rows == number, jnp.sum(used, axis=0, keepdims=True), weights)
    return jnp.concatenate([weights] * (TILE // pair.shape[1]), axis=1)


def put_weights(parity, weights, block):
    shifted = jnp.concatenate([weights[:, 1:], weights[:, :1]], axis=1)
    block[2 * PANEL :] = jnp.where(parity == 0, weights, shifted).astype(jnp.bfloat16)


def copy_all(source, out_ref, slot, sems):
    copies = [
        pltpu.make_async_copy(source, out_ref.at[at, slot], sems.at[at]) for at in range(out_ref.shape[0])
    ]
    for copy in copies:
        copy.start()
    return copies


def prepare_other(low_ref, b_ref, b_occ, stacks, counts, send_ref):
    low = low_ref[0]
    put_weights(1 - low, stack_weights(stacks, counts), send_ref)
    right_block(low, 1 - low, b_ref, b_occ, send_ref)


def prepare_own(low_ref, b_ref, b_occ, stacks, counts, a_ref, a_occ, out_ref, code_ref, own, sems):
    low = low_ref[0]
    put_weights(low, stack_weights(stacks, counts), own)
    right_block(low, low, b_ref, b_occ, own)
    copies = copy_all(own, out_ref, low, sems)
    for s in range(LEFT):
        held = a_ref[s].astype(jnp.float32) * a_occ[0, 0, 0, s].astype(jnp.float32)
        code_ref[0, s * TILE : (s + 1) * TILE] = encode(held)
    for copy in copies:
        copy.wait()


def add_other(low_ref, other, _, out_ref, sems):
    for copy in copy_all(other, out_ref, 1 - low_ref[0], sems):
        copy.wait()


def products(col_ref, code_hbm, b_ref, out_ref, code_ref, sems):
    n_cols = b_ref.shape[0]
    first = pltpu.make_async_copy(code_hbm.at[:4], code_ref.at[:4], sems.at[0])
    rest = pltpu.make_async_copy(code_hbm.at[4:], code_ref.at[4:], sems.at[1])
    first.start()
    rest.start()
    out_ref[...] = jnp.zeros_like(out_ref)
    lanes = lax.broadcasted_iota(jnp.int32, (W_ROWS, TILE), 1)
    weights = [b_ref[col_ref[0], q, 2 * PANEL :].astype(jnp.float32) for q in range(2)]

    first.wait()
    for g in range(n_cols):
        if g == 2:
            rest.wait()
        chosen = [
            [
                jnp.sum(jnp.where(lanes == 2 * (2 * g + at), weights[q], 0.0), axis=1, keepdims=True)
                for q in range(2)
            ]
            for at in range(2)
        ]

        def weighted(at, q, s, t):
            number = s * RIGHT + t
            weight = jnp.broadcast_to(chosen[at][q][number : number + 1], (16, TILE)).astype(jnp.bfloat16)
            row = at * PANEL + t * TILE
            tile = b_ref[g, q, row : row + TILE]
            return (tile.reshape(8, 16, TILE) * weight[None]).reshape(TILE, TILE)

        left = [
            [decode(code_ref[2 * g + at, s * TILE : (s + 1) * TILE]) for s in range(LEFT)]
            for at in range(2)
        ]
        for block, members in ((0, (0, 2)), (1, (1,))):
            lhs = jnp.concatenate([left[at][s] for at in range(2) for s in members], axis=1)
            extra = []
            for q in range(2):
                rhs = jnp.concatenate(
                    [
                        jnp.concatenate([weighted(at, q, s, 0), weighted(at, q, s, 1)], axis=1)
                        for at in range(2)
                        for s in members
                    ],
                    axis=0,
                )
                both = jnp.dot(lhs, rhs, preferred_element_type=jnp.float32)
                out_ref[2 * block, q] += both[:, :TILE]
                out_ref[2 * block + 1, q] += both[:, TILE:]
                extra.append(
                    jnp.concatenate([weighted(at, q, s, 2) for at in range(2) for s in members], axis=0)
                )
            both = jnp.dot(lhs, jnp.concatenate(extra, axis=1), preferred_element_type=jnp.float32)
            out_ref[2 * block, 0] += both[:, :TILE]
            out_ref[2 * block, 1] += both[:, TILE:]


def local(a_tiles, a_occ, b_tiles, b_occ, stacks, stack_count, c_keep):
    n_cols = lax.axis_size("col")
    vmem = pl.BlockSpec(memory_space=pltpu.VMEM)
    smem = pl.BlockSpec(memory_space=pltpu.SMEM)
    hbm = pl.BlockSpec(memory_space=pltpu.HBM)
    low = lax.axis_index("row_low").reshape(1)
    spread = jax.ShapeDtypeStruct((n_cols, 2, BLOCK, TILE), jnp.bfloat16)
    right_args = (
        b_tiles[:, 0, 0],
        b_occ.transpose(1, 3, 2, 0),
        stacks[0, 0, 0].transpose(2, 1, 0),
        stack_count,
    )
    send = pl.pallas_call(
        prepare_other,
        out_shape=jax.ShapeDtypeStruct((BLOCK, TILE), jnp.bfloat16),
        in_specs=[smem, vmem, smem, vmem, vmem],
        out_specs=vmem,
        name="prepare_other",
    )(low, *right_args)
    other = lax.ppermute(send, "row_low", [(0, 1), (1, 0)])
    right, codes = pl.pallas_call(
        prepare_own,
        out_shape=(spread, jax.ShapeDtypeStruct((1, PANEL, TILE), jnp.int16)),
        in_specs=[smem, vmem, smem, vmem, vmem, vmem, smem],
        out_specs=(hbm, vmem),
        scratch_shapes=[pltpu.VMEM((BLOCK, TILE), jnp.bfloat16), pltpu.SemaphoreType.DMA((n_cols,))],
        cost_estimate=pl.CostEstimate(flops=10_000_000, bytes_accessed=4_000_000, transcendentals=0),
        name="prepare_own",
    )(low, *right_args, a_tiles[0, 0, 0], a_occ)
    other, right, codes = lax.optimization_barrier((other, right, codes))
    right = pl.pallas_call(
        add_other,
        out_shape=spread,
        in_specs=[smem, vmem, hbm],
        out_specs=hbm,
        scratch_shapes=[pltpu.SemaphoreType.DMA((n_cols,))],
        input_output_aliases={2: 0},
        compiler_params=pltpu.CompilerParams(vmem_limit_bytes=54_000_000),
        name="add_other",
    )(low, other, right)
    right_all = lax.all_to_all(right, "col", 0, 0, tiled=True)
    left_all = lax.all_gather(codes, "row_high", axis=0, tiled=True)
    partial = pl.pallas_call(
        products,
        out_shape=pltpu.HBM((4, 2, TILE, TILE), jnp.float32),
        in_specs=[smem, hbm, vmem],
        out_specs=vmem,
        scratch_shapes=[pltpu.VMEM(left_all.shape, jnp.int16), pltpu.SemaphoreType.DMA((2,))],
        compiler_params=pltpu.CompilerParams(vmem_limit_bytes=16 * 1024 * 1024),
        name="products",
    )(
        lax.axis_index("col").reshape(1),
        pltpu.with_memory_space_constraint(left_all, pltpu.HBM),
        pltpu.with_memory_space_constraint(right_all, pltpu.VMEM),
    )
    shares = lax.all_to_all(
        partial.reshape(8, TILE, TILE), ("layer", "row_low"), 0, 0, tiled=True
    )
    kept = jnp.sum(shares, axis=0) * c_keep[0, 0, 0].astype(jnp.float32)
    return kept.astype(jnp.bfloat16)[None, None, None]


def solution(mesh):
    rows, cols, layers = (mesh.shape[name] for name in ("row", "col", "layer"))
    paired = Mesh(
        mesh.devices.reshape(rows // 2, 2, cols, layers), ("row_high", "row_low", "col", "layer")
    )
    row = ("row_high", "row_low")
    return jax.shard_map(
        local,
        mesh=paired,
        in_specs=(
            P("col", row, "layer", None, None, None),
            P("col", row, "layer", None),
            P("col", "layer", row, None, None, None),
            P("col", "layer", row, None),
            P("col", row, "layer", None, None, None),
            P("col", row, "layer", None),
            P("col", row, "layer"),
        ),
        out_specs=P("col", row, "layer", None, None),
        check_vma=False,
    )
```

```python
import jax
import jax.numpy as jnp
from jax import lax
from jax.experimental import pallas as pl
from jax.experimental.pallas import tpu as pltpu
from jax.sharding import Mesh, PartitionSpec as P

TILE = 128
LEFT = 3
RIGHT = 3
PANEL = LEFT * TILE
W_ROWS = 16
BLOCK = 2 * PANEL + W_ROWS


def encode(values):
    size = jnp.abs(values)
    least = 2.0**-124
    exponent = jnp.floor(jnp.log(jnp.maximum(size, least)) * 1.4426950408889634)
    scaled = size * jnp.exp2(-exponent)
    exponent = jnp.where(scaled >= 1.996, exponent + 1.0, jnp.where(scaled < 0.998, exponent - 1.0, exponent))
    exponent = jnp.maximum(exponent, -124.0)
    significand = jnp.floor(size * jnp.exp2(-exponent) * 128.0 + 0.5)
    significand = jnp.where(values < 0, -significand, significand)
    code = jnp.where(size < least, 0.0, (exponent + 61.0) * 512.0 + significand)
    return code.astype(jnp.int32).astype(jnp.int16)


def decode(codes):
    scaled = codes.astype(jnp.int32).astype(jnp.float32) * (1.0 / 128.0)
    exponent = jnp.floor(scaled * 0.25 + 0.5)
    return ((scaled - 4.0 * exponent) * jnp.exp2(exponent - 61.0)).astype(jnp.bfloat16)


def fetch_panels(parity, b_hbm, tiles, sems):
    copies = [
        pltpu.make_async_copy(b_hbm.at[2 * half + parity], tiles.at[half], sems.at[half])
        for half in range(2)
    ]
    for copy in copies:
        copy.start()
    return copies


def right_block(parity, tiles, b_occ, block):
    for half in range(2):
        for t in range(RIGHT):
            row = half * PANEL + t * TILE
            tile = tiles[half, t]
            held = b_occ[0, t, 0, 2 * half + parity] > 0
            block[row : row + TILE] = jnp.where(held, tile, jnp.zeros_like(tile))


def stack_weights(stacks, counts):
    pair = stacks[0] * RIGHT + stacks[1]
    live = lax.broadcasted_iota(jnp.int32, pair.shape, 0) < counts[0, 0]
    rows = lax.broadcasted_iota(jnp.int32, (W_ROWS, pair.shape[1]), 0)
    weights = jnp.zeros(rows.shape, jnp.float32)
    for number in range(LEFT * RIGHT):
        used = jnp.where(live & (pair == number), 1.0, 0.0)
        weights = jnp.where(rows == number, jnp.sum(used, axis=0, keepdims=True), weights)
    return jnp.concatenate([weights] * (TILE // pair.shape[1]), axis=1)


def put_weights(parity, weights, block):
    shifted = jnp.concatenate([weights[:, 1:], weights[:, :1]], axis=1)
    block[2 * PANEL :] = jnp.where(parity == 0, weights, shifted).astype(jnp.bfloat16)


def copy_all(source, out_ref, slot, sems):
    copies = [
        pltpu.make_async_copy(source, out_ref.at[at, slot], sems.at[at]) for at in range(out_ref.shape[0])
    ]
    for copy in copies:
        copy.start()
    return copies


def prepare_other(low_ref, b_hbm, b_occ, stacks, counts, send_ref, tiles, sems):
    parity = 1 - low_ref[0]
    copies = fetch_panels(parity, b_hbm, tiles, sems)
    put_weights(parity, stack_weights(stacks, counts), send_ref)
    for copy in copies:
        copy.wait()
    right_block(parity, tiles, b_occ, send_ref)


def prepare_own(
    low_ref, b_hbm, b_occ, stacks, counts, a_ref, a_occ, out_ref, code_ref, own, tiles, sems, out_sems
):
    parity = low_ref[0]
    copies = fetch_panels(parity, b_hbm, tiles, sems)
    put_weights(parity, stack_weights(stacks, counts), own)
    for copy in copies:
        copy.wait()
    right_block(parity, tiles, b_occ, own)
    copies = copy_all(own, out_ref, parity, out_sems)
    for s in range(LEFT):
        held = a_ref[s].astype(jnp.float32) * a_occ[0, 0, 0, s].astype(jnp.float32)
        code_ref[0, s * TILE : (s + 1) * TILE] = encode(held)
    for copy in copies:
        copy.wait()


def add_other(low_ref, other, _, out_ref, sems):
    for copy in copy_all(other, out_ref, 1 - low_ref[0], sems):
        copy.wait()


def products(col_ref, code_hbm, b_ref, out_ref, code_ref, sems):
    n_cols = b_ref.shape[0]
    copies = [
        pltpu.make_async_copy(code_hbm.at[pl.ds(2 * at, 2)], code_ref.at[pl.ds(2 * at, 2)], sems.at[at])
        for at in range(n_cols)
    ]
    for copy in copies:
        copy.start()
    out_ref[...] = jnp.zeros_like(out_ref)
    lanes = lax.broadcasted_iota(jnp.int32, (W_ROWS, TILE), 1)
    weights = [b_ref[col_ref[0], q, 2 * PANEL :].astype(jnp.float32) for q in range(2)]
    chosen = [
        [
            jnp.sum(jnp.where(lanes == 2 * panel, weights[q], 0.0), axis=1, keepdims=True)
            for q in range(2)
        ]
        for panel in range(2 * n_cols)
    ]

    copies[0].wait()
    for g in range(n_cols):
        if g == 1:
            for copy in copies[1:]:
                copy.wait()
        def weighted(at, q, s, t):
            number = s * RIGHT + t
            weight = jnp.broadcast_to(chosen[2 * g + at][q][number : number + 1], (16, TILE)).astype(jnp.bfloat16)
            row = at * PANEL + t * TILE
            tile = b_ref[g, q, row : row + TILE]
            return (tile.reshape(8, 16, TILE) * weight[None]).reshape(TILE, TILE)

        left = [
            [decode(code_ref[2 * g + at, s * TILE : (s + 1) * TILE]) for s in range(LEFT)]
            for at in range(2)
        ]
        for block, members in ((0, (0, 2)), (1, (1,))):
            lhs = jnp.concatenate([left[at][s] for at in range(2) for s in members], axis=1)
            extra = []
            for q in range(2):
                rhs = jnp.concatenate(
                    [
                        jnp.concatenate([weighted(at, q, s, 0), weighted(at, q, s, 1)], axis=1)
                        for at in range(2)
                        for s in members
                    ],
                    axis=0,
                )
                both = jnp.dot(lhs, rhs, preferred_element_type=jnp.float32)
                out_ref[2 * block, q] += both[:, :TILE]
                out_ref[2 * block + 1, q] += both[:, TILE:]
                extra.append(
                    jnp.concatenate([weighted(at, q, s, 2) for at in range(2) for s in members], axis=0)
                )
            both = jnp.dot(lhs, jnp.concatenate(extra, axis=1), preferred_element_type=jnp.float32)
            out_ref[2 * block, 0] += both[:, :TILE]
            out_ref[2 * block, 1] += both[:, TILE:]


def local(a_tiles, a_occ, b_tiles, b_occ, stacks, stack_count, c_keep):
    n_cols = lax.axis_size("col")
    vmem = pl.BlockSpec(memory_space=pltpu.VMEM)
    smem = pl.BlockSpec(memory_space=pltpu.SMEM)
    hbm = pl.BlockSpec(memory_space=pltpu.HBM)
    low = lax.axis_index("row_low").reshape(1)
    in_hbm = lambda array: pltpu.with_memory_space_constraint(array, pltpu.HBM)
    in_vmem = lambda array: pltpu.with_memory_space_constraint(array, pltpu.VMEM)
    params = pltpu.CompilerParams(vmem_limit_bytes=16 * 1024 * 1024)
    spread = pltpu.HBM((n_cols, 2, BLOCK, TILE), jnp.bfloat16)
    panels = [pltpu.VMEM((2, RIGHT, TILE, TILE), jnp.bfloat16), pltpu.SemaphoreType.DMA((2,))]
    right_args = (
        in_hbm(b_tiles[:, 0, 0]),
        in_hbm(b_occ.transpose(1, 3, 2, 0)),
        in_hbm(stacks[0, 0, 0].transpose(2, 1, 0)),
        in_hbm(stack_count),
    )
    send = pl.pallas_call(
        prepare_other,
        out_shape=pltpu.VMEM((BLOCK, TILE), jnp.bfloat16),
        in_specs=[smem, hbm, smem, vmem, vmem],
        out_specs=vmem,
        scratch_shapes=panels,
        compiler_params=params,
        name="prepare_other",
    )(low, *right_args)
    other = lax.ppermute(send, "row_low", [(0, 1), (1, 0)])
    right, codes = pl.pallas_call(
        prepare_own,
        out_shape=(spread, pltpu.HBM((1, PANEL, TILE), jnp.int16)),
        in_specs=[smem, hbm, smem, vmem, vmem, vmem, smem],
        out_specs=(hbm, vmem),
        scratch_shapes=[
            pltpu.VMEM((BLOCK, TILE), jnp.bfloat16),
            *panels,
            pltpu.SemaphoreType.DMA((n_cols,)),
        ],
        compiler_params=params,
        cost_estimate=pl.CostEstimate(flops=10_000_000, bytes_accessed=4_000_000, transcendentals=0),
        name="prepare_own",
    )(low, *right_args, in_hbm(a_tiles[0, 0, 0]), in_hbm(a_occ))
    other, right, codes = lax.optimization_barrier((other, right, codes))
    right = pl.pallas_call(
        add_other,
        out_shape=spread,
        in_specs=[smem, vmem, hbm],
        out_specs=hbm,
        scratch_shapes=[pltpu.SemaphoreType.DMA((n_cols,))],
        input_output_aliases={2: 0},
        compiler_params=params,
        name="add_other",
    )(low, in_vmem(other), in_hbm(right))
    right_all = lax.all_to_all(right, "col", 0, 0, tiled=True)
    left_all = lax.all_gather(codes, "row_high", axis=0, tiled=True)
    partial = pl.pallas_call(
        products,
        out_shape=pltpu.HBM((4, 2, TILE, TILE), jnp.float32),
        in_specs=[smem, hbm, vmem],
        out_specs=vmem,
        scratch_shapes=[pltpu.VMEM(left_all.shape, jnp.int16), pltpu.SemaphoreType.DMA((n_cols,))],
        compiler_params=params,
        name="products",
    )(
        lax.axis_index("col").reshape(1),
        in_hbm(left_all),
        in_vmem(right_all),
    )
    shares = lax.all_to_all(
        partial.reshape(8, TILE, TILE), ("layer", "row_low"), 0, 0, tiled=True
    )
    kept = jnp.sum(shares, axis=0) * c_keep[0, 0, 0].astype(jnp.float32)
    return kept.astype(jnp.bfloat16)[None, None, None]


def solution(mesh):
    rows, cols, layers = (mesh.shape[name] for name in ("row", "col", "layer"))
    paired = Mesh(
        mesh.devices.reshape(rows // 2, 2, cols, layers), ("row_high", "row_low", "col", "layer")
    )
    row = ("row_high", "row_low")
    return jax.shard_map(
        local,
        mesh=paired,
        in_specs=(
            P("col", row, "layer", None, None, None),
            P("col", row, "layer", None),
            P("col", "layer", row, None, None, None),
            P("col", "layer", row, None),
            P("col", row, "layer", None, None, None),
            P("col", row, "layer", None),
            P("col", row, "layer"),
        ),
        out_specs=P("col", row, "layer", None, None),
        check_vma=False,
    )
```
